512 devices in a mesh: samp: 16 (over z), var: 32 (over x, y, core).
Axes of the slice: x: 4, y: 4, z: 16, core: 2. Of those that a mesh axis runs over, the one named last changes fastest.
Arguments:
- dosage: bfloat16 [3072, 32768], P('samp', 'var'), may hold values from -5 to 5
- coefficients: bfloat16 [32768, 256], P('var'), as said below
- targets: bfloat16 [3072, 256], P('samp'), may hold values from -5 to 5
- mask_words: int32 [3072, 16], P('samp'), may hold values from 0 to 65535
- penalty: float32 [256], replicated, may hold values from 0.1 to 1.5
- past_steps: bfloat16 [8, 32768, 256], P(None, ('var', 'samp')), as said below
- past_changes: bfloat16 [8, 32768, 256], P(None, ('var', 'samp')), as said below
Outputs:
- updated: float32 [32768, 256], P(('var', 'samp'))
The draws below stay inside these ranges and needn't reach their ends.
Inputs may be any that keep to these rules, and one draw needn't show every extreme that they name: `past_changes`: each stored change y_i has a positive inner product with its own step s_i. `past_steps`: steps and changes come as pairs drawn together. The coefficients are drawn together with the stored pairs.
All inputs are finite; a program needn't handle non-finite values.
Results may differ from the reference program's by a relative error of at most 0.00066.
Values may be sent and summed in bfloat16 or wider, within the bound.
A program may use at most 64 MiB of HBM per device.

```python
import math
import jax
import jax.numpy as jnp
from jax import lax

K = 256
M = 8
NS = 3072
NV = 32768


def common_field(key):
    common_key = jax.random.fold_in(key, 101)
    return jax.random.normal(common_key, (1, NV, K), jnp.float32)


def history_pair(key):
    keys = [jax.random.fold_in(key, 101 + j) for j in range(6)]
    shape = (M, NV, K)
    common = common_field(key)
    own_part = jax.random.normal(keys[1], shape, jnp.float32)
    noise = jax.random.normal(keys[2], shape, jnp.float32)
    position = jnp.arange(NV, dtype=jnp.float32) / max(NV - 1, 1)
    row_scale = (1.0 + 2.0 * position)[None, :, None] * jnp.exp(jax.random.uniform(keys[3], (1, NV, 1), jnp.float32, 0.0, math.log(10.0)))
    col_scale = jnp.exp(jax.random.uniform(keys[4], (1, 1, K), jnp.float32, 0.0, math.log(10.0)))
    factor = jnp.exp(jax.random.uniform(keys[5], (M, 1, 1), jnp.float32, math.log(0.5), math.log(4.0)))
    spread = row_scale * col_scale / 30.0
    steps = spread * (0.6 * common + own_part)
    changes = factor * steps + 0.5 * spread * noise
    return (steps, changes)


def draw_coefficients(key, part):
    shared = common_field(key)[0]
    fresh_key = jax.random.fold_in(key, 131)
    fresh = jax.random.normal(fresh_key, (NV, K), jnp.float32)
    return (0.8 * shared + 0.6 * fresh).astype(jnp.bfloat16)


def draw_past_steps(key, part):
    return history_pair(key)[0].astype(jnp.bfloat16)


def draw_past_changes(key, part):
    return history_pair(key)[1].astype(jnp.bfloat16)


def with_ends(array, key, smallest, high):
    index_at = [jax.random.randint(jax.random.fold_in(key, axis), (), 0, length) for axis, length in enumerate(array.shape)]
    widest = array.shape.index(max(array.shape))
    beside = index_at[:widest] + [(index_at[widest] + 1) % array.shape[widest]] + index_at[widest + 1:]
    return array.at[tuple(index_at)].set(smallest).at[tuple(beside)].set(high)


def with_spikes(array, rng, source, target, blocks, factor):
    def block_of(axis_at):
        return (jnp.arange(array.shape[axis_at]) // (array.shape[axis_at] // blocks)).reshape((-1,) + (1,) * (array.ndim - 1 - axis_at))

    first = jax.random.permutation(rng, blocks)[block_of(target)]
    second = (block_of(target) + blocks // 2) % blocks
    return jnp.where((block_of(source) == first) | (block_of(source) == second), factor * array, array)


def level_of(key, shape, pieces, least, top_value):
    level, own = 1.0, jax.random.fold_in(key, 6)
    for dim, parts in pieces:
        heights = jnp.exp(jax.random.uniform(jax.random.fold_in(own, dim), (parts,), jnp.float32, least / len(pieces), top_value / len(pieces)))
        level = level * jnp.repeat(heights, shape[dim] // parts).reshape([-1 if axis == dim else 1 for axis in range(len(shape))])
    return level


def gaussian(key, shape, scale, most, cuts=(), held_as=jnp.bfloat16):
    values = jax.random.normal(key, shape, jnp.float32) * scale
    if len(cuts) > 0:
        values = level_of(key, shape, cuts, -0.22, 0.18) * values
    return jnp.clip(values, min=-most, max=most).astype(held_as)


def noise_with(stream_key, dims, scale, most, shards, heavy, held_as=jnp.bfloat16):
    drawn = scale * jax.random.normal(stream_key, dims, jnp.float32)
    if shards:
        drawn = drawn * level_of(stream_key, dims, shards, -0.22, 0.18)
    return jnp.clip(with_spikes(drawn, jax.random.fold_in(stream_key, 3), *heavy), -most, most).astype(held_as)


def setup_inputs(seed: int = 0) -> dict:
    streams_of = jax.random.split(jax.random.key(seed), 8)
    return {
        "dosage": noise_with(streams_of[0], (NS, NV), 1.0, 5.0, ((0, 16), (1, 32)), (0, 1, 32, 2.75)),
        "coefficients": draw_coefficients(jax.random.fold_in(streams_of[7], 71), 0),
        "targets": gaussian(streams_of[2], (NS, K), 1.0, 5.0, ((0, 16),)),
        "mask_words": with_ends(jax.random.randint(streams_of[3], (NS, K // 16), 0, 65536), jax.random.fold_in(streams_of[3], 1), 0, 65535).astype(jnp.int32),
        "penalty": jnp.clip(jnp.exp(jax.random.uniform(streams_of[4], (K,), jnp.float32, math.log(0.1), math.log(1.5))), 0.1, 1.5),
        "past_steps": draw_past_steps(jax.random.fold_in(streams_of[7], 71), 0),
        "past_changes": draw_past_changes(jax.random.fold_in(streams_of[7], 71), 0),
    }


step_size = 0.5


def unpack_mask(mask_words):
    shifts = jnp.arange(16, dtype=jnp.int32)
    flags = jnp.bitwise_and(jnp.right_shift(mask_words[:, :, None], shifts[None, None, :]), 1)
    return flags.reshape(mask_words.shape[0], -1).astype(jnp.float32)


def solve_upper(upper, right):
    count = right.shape[0]
    values = [None] * count
    for i in reversed(range(count)):
        total = right[i]
        for j in range(i + 1, count):
            total = total - upper[i, j] * values[j]
        values[i] = total / upper[i, i]
    return jnp.stack(values)


def solve_upper_transposed(upper, right):
    count = right.shape[0]
    values = [None] * count
    for i in range(count):
        total = right[i]
        for j in range(i):
            total = total - upper[j, i] * values[j]
        values[i] = total / upper[i, i]
    return jnp.stack(values)


def compact_weights(cross, change_gram, step_dots, change_dots):
    count = cross.shape[0]
    scaling = cross[count - 1, count - 1] / change_gram[count - 1, count - 1]
    upper = jnp.triu(cross)
    diagonal = jnp.diagonal(cross)
    inner_u = solve_upper(upper, step_dots)
    inside = diagonal * inner_u + scaling * jnp.dot(change_gram, inner_u, precision=lax.Precision.HIGHEST) - scaling * change_dots
    outer_p = solve_upper_transposed(upper, inside)
    return scaling, inner_u, outer_p


def reference(dosage, coefficients, targets, mask_words, penalty, past_steps, past_changes):
    scale = NV ** -0.5
    observed = unpack_mask(mask_words)
    margin = jnp.dot(dosage, coefficients, preferred_element_type=jnp.float32) * scale
    residual = (observed * (margin - targets.astype(jnp.float32))).astype(jnp.bfloat16)
    gradient = lax.dot_general(dosage, residual, (((0,), (0,)), ((), ())), preferred_element_type=jnp.float32) * scale
    steps_wide = past_steps.astype(jnp.float32)
    changes_wide = past_changes.astype(jnp.float32)
    high = lax.Precision.HIGHEST
    cross = jnp.einsum('mvk,nvk->mn', steps_wide, changes_wide, precision=high)
    change_gram = jnp.einsum('mvk,nvk->mn', changes_wide, changes_wide, precision=high)
    step_dots = jnp.einsum('mvk,vk->m', steps_wide, gradient, precision=high)
    change_dots = jnp.einsum('mvk,vk->m', changes_wide, gradient, precision=high)
    scaling, inner_u, outer_p = compact_weights(cross, change_gram, step_dots, change_dots)
    direction = scaling * gradient + jnp.einsum('m,mvk->vk', outer_p, steps_wide, precision=high) - scaling * jnp.einsum('m,mvk->vk', inner_u, changes_wide, precision=high)
    moved = coefficients.astype(jnp.float32) - step_size * direction
    limit = step_size * penalty[None, :]
    return moved - jnp.clip(moved, -limit, limit)
```

```python
import functools

import jax
import jax.numpy as jnp
from jax import lax
from jax.experimental import pallas as pl
from jax.experimental.pallas import tpu as pltpu
from jax.sharding import PartitionSpec as P

MESH = pl.DeviceIdType.MESH
STEP = 0.5
ZN = 16
VN = 32
PAIRS = 8
UNITS = 12
OFFSET = [0] + [(s + 1) // 2 if s % 2 else -(s // 2) for s in range(1, ZN)]
GROUPS = [(0, 4), (4, 4), (8, 4), (12, 4)]
EARLY = 9


def wait_for(ref, sem):
    pltpu.make_async_copy(ref, ref, sem).wait()


def row_sum(block):
    return jnp.sum(block, axis=0)


def pair_index(i, j):
    return i * PAIRS - (i * (i - 1)) // 2 + (j - i)


def weight_rows(sums):
    lane = lax.broadcasted_iota(jnp.int32, (1, 128), 1)

    def entry(k):
        return jnp.broadcast_to(sums[:, k : k + 1], (1, 128))

    def unit(k):
        return jnp.where(lane == k, 1.0, 0.0)

    half = PAIRS * (PAIRS + 1) // 2
    upper = {(i, j): entry(pair_index(i, j)) for i in range(PAIRS) for j in range(i, PAIRS)}
    gram = {(i, j): entry(half + pair_index(i, j)) for i in range(PAIRS) for j in range(i, PAIRS)}
    scaling = upper[PAIRS - 1, PAIRS - 1] / gram[PAIRS - 1, PAIRS - 1]
    inner = [None] * PAIRS
    for i in reversed(range(PAIRS)):
        total = unit(i)
        for j in range(i + 1, PAIRS):
            total = total - upper[i, j] * inner[j]
        inner[i] = total / upper[i, i]
    outer = [None] * PAIRS
    for i in range(PAIRS):
        total = gram[min(i, 0), max(i, 0)] * inner[0]
        for j in range(1, PAIRS):
            total = total + gram[min(i, j), max(i, j)] * inner[j]
        total = upper[i, i] * inner[i] + scaling * total - scaling * unit(PAIRS + i)
        for j in range(i):
            total = total - upper[j, i] * outer[j]
        outer[i] = total / upper[i, i]
    return scaling, outer + [-scaling * row for row in inner]


def kernel(
    dosage_hbm,
    coef_hbm,
    target_hbm,
    mask_hbm,
    penalty_ref,
    steps_hbm,
    changes_hbm,
    out_ref,
    dosage,
    coef,
    target,
    mask,
    hist,
    part,
    tiles,
    x_all,
    x_turned,
    r_all,
    partial_in,
    hist_other,
    gram_acc,
    gram_own,
    gram_plane,
    gram_line,
    weights,
    gamma,
    g_acc,
    g_half,
    g_own,
    dots_own,
    dots_line,
    dots_mid,
    dots_plane,
    local_sem,
    part_send,
    part_recv,
    dose_send,
    dose_recv,
    swap_send,
    swap_recv,
    hist_send,
    hist_recv,
    gram_send,
    gram_recv,
    line_send,
    line_recv,
    res_send,
    res_recv,
    g_send,
    g_recv,
    dots_send,
    dots_recv,
):
    z = lax.axis_index("samp")
    v = lax.axis_index("var")
    core = lax.rem(v, 2)
    chip = lax.div(v, 2)
    other = 1 - core
    mate = v + 1 - 2 * core
    scale = (VN * dosage.shape[1]) ** -0.5

    def unit_of(c):
        x, y = lax.div(c, 4), lax.rem(c, 4)
        s = lax.rem(x + y, 4)
        return s < 3, 3 * x + jnp.minimum(s, 2)

    owner, mine = unit_of(chip)
    lanes = pl.ds(pl.multiple_of(core * 128, 128), 128)
    other_lanes = pl.ds(pl.multiple_of(other * 128, 128), 128)

    def at_z(s):
        return lax.rem(z - OFFSET[s] + ZN, ZN)

    def remote(src, dst, send, recv, zz, vv):
        return pltpu.make_async_remote_copy(
            src_ref=src, dst_ref=dst, send_sem=send, recv_sem=recv, device_id=(zz, vv), device_id_type=MESH
        )

    loads = [
        pltpu.make_async_copy(dosage_hbm, dosage, local_sem.at[0]),
        pltpu.make_async_copy(coef_hbm, coef, local_sem.at[1]),
        pltpu.make_async_copy(steps_hbm, hist.at[pl.ds(0, PAIRS)], local_sem.at[2]),
        pltpu.make_async_copy(changes_hbm, hist.at[pl.ds(PAIRS, PAIRS)], local_sem.at[3]),
        pltpu.make_async_copy(target_hbm, target, local_sem.at[4]),
        pltpu.make_async_copy(mask_hbm, mask, local_sem.at[5]),
    ]
    for load in loads:
        load.start()

    barrier = pltpu.get_barrier_semaphore()

    @pl.loop(1, VN)
    def _(r):
        pl.semaphore_signal(barrier, inc=1, device_id=(z, lax.rem(v + r, VN)), device_id_type=MESH)

    @pl.loop(1, ZN)
    def _(r):
        pl.semaphore_signal(barrier, inc=1, device_id=(lax.rem(z + r, ZN), v), device_id_type=MESH)

    loads[0].wait()
    loads[1].wait()
    product = jnp.dot(dosage[...], coef[...], preferred_element_type=jnp.float32)
    for u in range(UNITS):
        for h in range(2):
            part[u, h] = product[16 * u : 16 * u + 16, 128 * h : 128 * h + 128]
    for j in range(ZN // 2):
        top = dosage[0:96, 128 * j : 128 * j + 128]
        low = dosage[96:192, 128 * j : 128 * j + 128]
        tiles[2 * j] = jnp.concatenate([top[:, :64], low[:, :64]], axis=1)
        tiles[2 * j + 1] = jnp.concatenate([top[:, 64:], low[:, 64:]], axis=1)
    loads[2].wait()
    loads[3].wait()

    pl.semaphore_wait(barrier, VN - 1 + ZN - 1)

    @pl.loop(1, VN)
    def _(r):
        dest = lax.rem(v + r, VN)
        owns, u = unit_of(lax.div(dest, 2))

        @pl.when(owns)
        def _():
            remote(part.at[u, lax.rem(dest, 2)], partial_in.at[VN - 1 - r], part_send, part_recv, z, dest).start()

    def send_dosage(s):
        g = s // 4
        remote(tiles.at[at_z(s)], x_all.at[core, s], dose_send, dose_recv.at[g], at_z(s), v).start()

    for s in range(1, EARLY):
        send_dosage(s)
    hist_copy = remote(hist.at[:, :, other_lanes], hist_other, hist_send, hist_recv, z, mate)
    hist_copy.start()

    gram_acc[...] = jnp.zeros_like(gram_acc)
    half = PAIRS * (PAIRS + 1) // 2

    @pl.loop(0, 8)
    def _(t):
        rows = pl.ds(pl.multiple_of(lax.div(t, 2) * 16, 16), 16)
        cols = pl.ds(pl.multiple_of(lax.rem(t, 2) * 128, 128), 128)
        wide = [hist[i, rows, cols].astype(jnp.float32) for i in range(2 * PAIRS)]
        for i in range(PAIRS):
            for j in range(i, PAIRS):
                k = pair_index(i, j)
                one = wide[i] * wide[PAIRS + j]
                two = wide[PAIRS + i] * wide[PAIRS + j]
                gram_acc[k] += one[:8] + one[8:]
                gram_acc[half + k] += two[:8] + two[8:]

    folded = jnp.sum(gram_acc[...], axis=1)
    gram_own[0] = lax.dot_general(
        jnp.ones((8, 128), jnp.float32),
        folded,
        (((1,), (1,)), ((), ())),
        precision=lax.Precision.HIGHEST,
        preferred_element_type=jnp.float32,
    )[0:1]

    @pl.loop(1, VN)
    def _(r):
        remote(
            gram_own.at[0], gram_plane.at[VN - 1 - r], gram_send, gram_recv, z, lax.rem(v + r, VN)
        ).start()

    x_all[core, 0] = tiles[z]
    loads[4].wait()
    loads[5].wait()

    def spread(groups_from, count, g):
        @pl.loop(1, VN // 2)
        def _(r):
            block = r_all.at[pl.ds(groups_from, count), mine]
            remote(block, block, res_send.at[1], res_recv.at[4 + g], z, lax.rem(v + 2 * r, VN)).start()

    @pl.when(owner)
    def _():
        rows = pl.ds(pl.multiple_of(mine * 16, 16), 16)
        lane = lax.broadcasted_iota(jnp.int32, (16, 128), 1)
        word_at = jnp.right_shift(lane, 4) + 8 * core
        words = mask[rows, :]
        word = jnp.zeros((16, 128), jnp.int32)
        for w in range(16):
            word = jnp.where(word_at == w, jnp.broadcast_to(words[:, w : w + 1], (16, 128)), word)
        observed = jnp.bitwise_and(jnp.right_shift(word, jnp.bitwise_and(lane, 15)), 1).astype(jnp.float32)
        wanted = target[rows, lanes].astype(jnp.float32)
        wait_for(partial_in, part_recv)
        margin = (row_sum(partial_in[...]) + part[mine, core]) * scale
        r_all[0, mine] = (observed * (margin - wanted)).astype(jnp.bfloat16)
        for s in range(1, ZN):
            remote(r_all.at[0, mine], r_all.at[s, mine], res_send.at[0], res_recv.at[s // 4], at_z(s), v).start()
        spread(0, 1, 0)

    for s in range(EARLY, ZN):
        send_dosage(s)

    wait_for(gram_plane, gram_recv)
    gram_own[1] = row_sum(gram_plane[...]) + gram_own[0]
    for s in range(1, ZN):
        remote(gram_own.at[1], gram_line.at[s - 1], line_send.at[0], line_recv.at[0], at_z(s), v).start()

    def swap(g):
        first, count = GROUPS[g]
        skip = 1 if g == 0 else 0
        wait_for(x_all.at[core, pl.ds(first + skip, count - skip)], dose_recv.at[g])
        block = x_all.at[core, pl.ds(first, count)]
        remote(block, block, swap_send, swap_recv.at[g], z, mate).start()

    def pass_on(g):
        first, count = GROUPS[g]
        skip = 1 if g == 0 else 0

        @pl.when(owner)
        def _():
            wait_for(r_all.at[pl.ds(first + skip, count - skip), mine], res_recv.at[g])
            spread(first + skip, count - skip, g + 1)

    def turn(g):
        first, count = GROUPS[g]
        wait_for(x_all.at[other, pl.ds(first, count)], swap_recv.at[g])
        for c in range(2):
            x_turned[c, g] = x_all[c, first : first + count].reshape(count * 96, 128).T

    def residuals_here(first, count, g):
        @pl.when(owner)
        def _():
            wait_for(r_all.at[pl.ds(first, count), pl.ds(0, UNITS - 1)], res_recv.at[4 + g])

        @pl.when(jnp.logical_not(owner))
        def _():
            wait_for(r_all.at[pl.ds(first, count)], res_recv.at[4 + g])

    def multiply(g):
        first, count = GROUPS[g]
        if g == 0:
            residuals_here(0, 1, 0)
            residuals_here(1, count - 1, 1)
        else:
            residuals_here(first, count, g + 1)
        rows = jnp.concatenate(
            [
                r_all[first : first + count, 0:6].reshape(count * 96, 128),
                r_all[first : first + count, 6:12].reshape(count * 96, 128),
            ],
            axis=1,
        )
        for c in range(2):
            total = jnp.dot(x_turned[c, g], rows, preferred_element_type=jnp.float32)
            g_acc[c] = total if g == 0 else g_acc[c] + total

    swap(0)
    swap(1)
    pass_on(0)
    pass_on(1)
    turn(0)
    pass_on(2)
    turn(1)
    pass_on(3)
    multiply(0)
    multiply(1)
    swap(2)
    swap(3)
    turn(2)
    multiply(2)
    turn(3)
    multiply(3)

    for c in range(2):
        total = g_acc[c]
        g_half[c] = (total[:64, :128] + total[64:, 128:]) * scale
    g_copy = remote(g_half.at[other], g_own.at[core], g_send, g_recv, z, mate)
    g_copy.start()
    g_own[core] = g_half[core]

    near, far = g_half[core], g_half[other]
    hist_copy.wait_recv()
    sub = lax.broadcasted_iota(jnp.int32, (16, 128), 0)
    lane = lax.broadcasted_iota(jnp.int32, (16, 128), 1)
    folds = []
    for i in range(2 * PAIRS):
        both = hist[i, :, lanes].astype(jnp.float32) * near + hist_other[i].astype(jnp.float32) * far
        folds.append(jnp.sum(both, axis=0, keepdims=True))
    sums = jnp.sum(jnp.concatenate(folds, axis=0), axis=1, keepdims=True)
    dots_own[0] = jnp.sum(jnp.where(sub == lane, sums, 0.0), axis=0, keepdims=True)
    for s in range(1, ZN):
        remote(dots_own.at[0], dots_line.at[s - 1], line_send.at[1], line_recv.at[1], at_z(s), v).start()

    wait_for(gram_line, line_recv.at[0])
    scaling, rows = weight_rows(row_sum(gram_line[...]) + gram_own[1])
    gamma[...] = scaling
    for i in range(2 * PAIRS):
        weights[i : i + 1, :] = rows[i]
    g_copy.wait_recv()

    wait_for(dots_line, line_recv.at[1])
    dots_mid[0] = row_sum(dots_line[...]) + dots_own[0]

    @pl.loop(1, VN)
    def _(r):
        remote(
            dots_mid.at[0], dots_plane.at[VN - 1 - r], dots_send, dots_recv, z, lax.rem(v + r, VN)
        ).start()

    own_rows = pl.ds(pl.multiple_of(z * 64, 64), 64)
    start = coef[own_rows, :].astype(jnp.float32)
    gradient = jnp.concatenate([g_own[0], g_own[1]], axis=1)
    start = start - STEP * (gamma[0:1, 0:1] * gradient)
    limit = STEP * penalty_ref[...]

    wait_for(dots_plane, dots_recv)
    dots = row_sum(dots_plane[...]) + dots_mid[0]
    mix = jnp.sum(weights[...] * dots, axis=1, keepdims=True)
    along = mix[0:1] * hist[0].astype(jnp.float32)
    for i in range(1, 2 * PAIRS):
        along = along + mix[i : i + 1] * hist[i].astype(jnp.float32)
    moved = start - STEP * along
    out_ref[...] = moved - jnp.clip(moved, -limit, limit)

    @pl.when(owner)
    def _():
        wait_for(part.at[pl.ds(0, UNITS - 1)], part_send)
        wait_for(part.at[0, 0], part_send)
        wait_for(r_all.at[pl.ds(1, ZN - 1), 0], res_send.at[0])
        wait_for(r_all.at[pl.ds(0, ZN - 1), 0], res_send.at[1])
        for _ in range(ZN - 1):
            wait_for(r_all.at[pl.ds(1, ZN - 1), 0], res_send.at[1])

    @pl.when(jnp.logical_not(owner))
    def _():
        wait_for(part, part_send)

    wait_for(tiles.at[pl.ds(1, ZN - 1)], dose_send)
    wait_for(x_all.at[0], swap_send)
    hist_copy.wait_send()
    g_copy.wait_send()
    wait_for(gram_plane, gram_send)
    wait_for(gram_line, line_send.at[0])
    wait_for(dots_line, line_send.at[1])
    wait_for(dots_plane, dots_send)


def per_device(dosage, coefficients, targets, mask_words, penalty, past_steps, past_changes):
    samples, variants = dosage.shape
    traits = coefficients.shape[1]
    owned = variants // ZN
    f32, bf16 = jnp.float32, jnp.bfloat16
    vmem = pltpu.VMEM
    dma = pltpu.SemaphoreType.DMA
    anywhere = pl.BlockSpec(memory_space=pl.ANY)
    return pl.pallas_call(
        kernel,
        out_shape=jax.ShapeDtypeStruct((owned, traits), f32),
        in_specs=[anywhere] * 4 + [pl.BlockSpec(memory_space=vmem)] + [anywhere] * 2,
        out_specs=pl.BlockSpec(memory_space=vmem),
        scratch_shapes=[
            vmem((samples, variants), bf16),
            vmem((variants, traits), bf16),
            vmem((samples, traits), bf16),
            vmem(mask_words.shape, jnp.int32),
            vmem((2 * PAIRS, owned, traits), bf16),
            vmem((UNITS, 2, 16, 128), f32),
            vmem((ZN, 96, 128), bf16),
            vmem((2, ZN, 96, 128), bf16),
            vmem((2, 4, 128, 384), bf16),
            vmem((ZN, UNITS, 16, 128), bf16),
            vmem((VN - 1, 16, 128), f32),
            vmem((2 * PAIRS, owned, 128), bf16),
            vmem((128, 8, 128), f32),
            vmem((2, 1, 128), f32),
            vmem((VN - 1, 1, 128), f32),
            vmem((ZN - 1, 1, 128), f32),
            vmem((2 * PAIRS, 128), f32),
            vmem((1, 128), f32),
            vmem((2, 128, 256), f32),
            vmem((2, owned, 128), f32),
            vmem((2, owned, 128), f32),
            vmem((1, 1, 128), f32),
            vmem((ZN - 1, 1, 128), f32),
            vmem((1, 1, 128), f32),
            vmem((VN - 1, 1, 128), f32),
            dma((6,)),
            dma,
            dma,
            dma,
            dma((4,)),
            dma,
            dma((4,)),
            dma,
            dma,
            dma,
            dma,
            dma((2,)),
            dma((2,)),
            dma((2,)),
            dma((9,)),
            dma,
            dma,
            dma,
            dma,
        ],
        compiler_params=pltpu.CompilerParams(
            collective_id=0, has_side_effects=True, vmem_limit_bytes=48 * 1024 * 1024
        ),
    )(dosage, coefficients, targets, mask_words, penalty[None, :], past_steps, past_changes)


def solution(mesh):
    in_specs = (
        P("samp", "var"),
        P("var", None),
        P("samp", None),
        P("samp", None),
        P(),
        P(None, ("var", "samp"), None),
        P(None, ("var", "samp"), None),
    )
    out_specs = P(("var", "samp"), None)
    return jax.shard_map(
        per_device, mesh=mesh, in_specs=in_specs, out_specs=out_specs, check_vma=False
    )
```

```python
import functools

import jax
import jax.numpy as jnp
from jax import lax
from jax.experimental import pallas as pl
from jax.experimental.pallas import tpu as pltpu
from jax.sharding import PartitionSpec as P

MESH = pl.DeviceIdType.MESH
STEP = 0.5
ZN = 16
VN = 32
PAIRS = 8
UNITS = 12
OFFSET = [0] + [(s + 1) // 2 if s % 2 else -(s // 2) for s in range(1, ZN)]
GROUPS = [(0, 4), (4, 4), (8, 4), (12, 4)]
SENDS = {"near": (8, 7, 6, 5, 4, 3, 2, 1), "pre": (15,), "post": (), 0: (14, 13), 1: (12, 11, 10, 9), 2: (), 3: ()}
ORDER = (0, 1, 3, 2)


def wait_for(ref, sem):
    pltpu.make_async_copy(ref, ref, sem).wait()


def row_sum(block):
    return jnp.sum(block, axis=0)


def pair_index(i, j):
    return i * PAIRS - (i * (i - 1)) // 2 + (j - i)


def weight_rows(sums):
    lane = lax.broadcasted_iota(jnp.int32, (1, 128), 1)

    def entry(k):
        return jnp.broadcast_to(sums[:, k : k + 1], (1, 128))

    def unit(k):
        return jnp.where(lane == k, 1.0, 0.0)

    half = PAIRS * (PAIRS + 1) // 2
    upper = {(i, j): entry(pair_index(i, j)) for i in range(PAIRS) for j in range(i, PAIRS)}
    gram = {(i, j): entry(half + pair_index(i, j)) for i in range(PAIRS) for j in range(i, PAIRS)}
    scaling = upper[PAIRS - 1, PAIRS - 1] / gram[PAIRS - 1, PAIRS - 1]
    inner = [None] * PAIRS
    for i in reversed(range(PAIRS)):
        total = unit(i)
        for j in range(i + 1, PAIRS):
            total = total - upper[i, j] * inner[j]
        inner[i] = total / upper[i, i]
    outer = [None] * PAIRS
    for i in range(PAIRS):
        total = gram[min(i, 0), max(i, 0)] * inner[0]
        for j in range(1, PAIRS):
            total = total + gram[min(i, j), max(i, j)] * inner[j]
        total = upper[i, i] * inner[i] + scaling * total - scaling * unit(PAIRS + i)
        for j in range(i):
            total = total - upper[j, i] * outer[j]
        outer[i] = total / upper[i, i]
    return scaling, outer + [-scaling * row for row in inner]


def kernel(
    dosage_hbm,
    coef_hbm,
    target_hbm,
    mask_hbm,
    penalty_ref,
    steps_hbm,
    changes_hbm,
    out_ref,
    dosage,
    coef,
    target,
    mask,
    mask_rows,
    hist,
    part,
    tiles,
    x_all,
    x_turned,
    r_all,
    partial_in,
    hist_other,
    gram_acc,
    gram_own,
    gram_plane,
    gram_line,
    weights,
    gamma,
    g_acc,
    g_half,
    g_own,
    dots_own,
    dots_line,
    dots_mid,
    dots_plane,
    local_sem,
    part_send,
    part_recv,
    dose_send,
    dose_recv,
    swap_send,
    swap_recv,
    hist_send,
    hist_recv,
    gram_send,
    gram_recv,
    line_send,
    line_recv,
    res_send,
    res_recv,
    g_send,
    g_recv,
    dots_send,
    dots_recv,
    beyond,
):
    z = lax.axis_index("samp")
    v = lax.axis_index("var")
    core = lax.rem(v, 2)
    chip = lax.div(v, 2)
    other = 1 - core
    mate = v + 1 - 2 * core
    scale = (VN * dosage.shape[1]) ** -0.5

    def unit_of(c):
        x, y = lax.div(c, 4), lax.rem(c, 4)
        s = lax.rem(x + y, 4)
        return s < 3, 3 * x + jnp.minimum(s, 2)

    owner, mine = unit_of(chip)
    lanes = pl.ds(pl.multiple_of(core * 128, 128), 128)
    other_lanes = pl.ds(pl.multiple_of(other * 128, 128), 128)

    def at_z(s):
        return lax.rem(z - OFFSET[s] + ZN, ZN)

    def remote(src, dst, send, recv, zz, vv):
        return pltpu.make_async_remote_copy(
            src_ref=src, dst_ref=dst, send_sem=send, recv_sem=recv, device_id=(zz, vv), device_id_type=MESH
        )

    coming, leaving = {}, []

    def take(name):
        coming.pop(name)()

    def finish():
        for name in list(coming):
            take(name)
        for left in leaving:
            left()

    barrier = pltpu.get_barrier_semaphore()

    for r in (4, 12, 3, 13, 2, 14, 1, 15):
        pl.semaphore_signal(barrier, inc=1, device_id=(lax.rem(z + r, ZN), v), device_id_type=MESH)

    @pl.loop(1, VN)
    def _(r):
        pl.semaphore_signal(barrier, inc=1, device_id=(z, lax.rem(v + r, VN)), device_id_type=MESH)

    loads = [
        pltpu.make_async_copy(dosage_hbm, dosage, local_sem.at[0]),
        pltpu.make_async_copy(coef_hbm, coef, local_sem.at[1]),
        pltpu.make_async_copy(steps_hbm, hist.at[pl.ds(0, PAIRS)], local_sem.at[2]),
        pltpu.make_async_copy(changes_hbm, hist.at[pl.ds(PAIRS, PAIRS)], local_sem.at[3]),
        pltpu.make_async_copy(target_hbm, target, local_sem.at[4]),
        pltpu.make_async_copy(mask_hbm, mask, local_sem.at[5]),
    ]
    for load in loads:
        load.start()

    loads[0].wait()
    loads[1].wait()
    product = jnp.dot(dosage[...], coef[...], preferred_element_type=jnp.float32)
    for u in range(UNITS):
        for h in range(2):
            part[u, h] = product[16 * u : 16 * u + 16, 128 * h : 128 * h + 128]
    for j in range(ZN // 2):
        top = dosage[0:96, 128 * j : 128 * j + 128]
        low = dosage[96:192, 128 * j : 128 * j + 128]
        tiles[2 * j] = jnp.concatenate([top[:, :64], low[:, :64]], axis=1)
        tiles[2 * j + 1] = jnp.concatenate([top[:, 64:], low[:, 64:]], axis=1)
    for load in loads[2:]:
        load.wait()
    mask_rows[...] = mask[...].astype(jnp.float32).T

    pl.semaphore_wait(barrier, VN - 1 + 8)
    for r in (4, 12):
        pl.semaphore_signal(beyond, inc=1, device_id=(lax.rem(z + r, ZN), v), device_id_type=MESH)

    @pl.loop(1, VN)
    def _(r):
        dest = lax.rem(v + r, VN)
        owns, u = unit_of(lax.div(dest, 2))

        @pl.when(owns)
        def _():
            remote(part.at[u, lax.rem(dest, 2)], partial_in.at[VN - 1 - r], part_send, part_recv, z, dest).start()

    def part_left():
        @pl.when(owner)
        def _():
            wait_for(part.at[pl.ds(0, UNITS - 1)], part_send)
            wait_for(part.at[0, 0], part_send)

        @pl.when(jnp.logical_not(owner))
        def _():
            wait_for(part, part_send)

    def part_here():
        @pl.when(owner)
        def _():
            wait_for(partial_in, part_recv)

    leaving.append(part_left)
    coming["part"] = part_here

    def send_dosage(s):
        g = s // 4
        remote(tiles.at[at_z(s)], x_all.at[core, s], dose_send, dose_recv.at[g], at_z(s), v).start()
        leaving.append(lambda: wait_for(tiles.at[0], dose_send))

    def dosage_here(g):
        first, count = GROUPS[g]
        skip = 1 if g == 0 else 0
        wait_for(x_all.at[core, pl.ds(first + skip, count - skip)], dose_recv.at[g])

    for s in SENDS["near"]:
        send_dosage(s)
    for g in range(4):
        coming["dose%d" % g] = functools.partial(dosage_here, g)
    hist_copy = remote(hist.at[:, :, other_lanes], hist_other, hist_send, hist_recv, z, mate)
    hist_copy.start()
    leaving.append(hist_copy.wait_send)
    coming["hist"] = hist_copy.wait_recv

    gram_acc[...] = jnp.zeros_like(gram_acc)
    half = PAIRS * (PAIRS + 1) // 2

    @pl.loop(0, 8)
    def _(t):
        rows = pl.ds(pl.multiple_of(lax.div(t, 2) * 16, 16), 16)
        cols = pl.ds(pl.multiple_of(lax.rem(t, 2) * 128, 128), 128)
        wide = [hist[i, rows, cols].astype(jnp.float32) for i in range(2 * PAIRS)]
        for i in range(PAIRS):
            for j in range(i, PAIRS):
                k = pair_index(i, j)
                one = wide[i] * wide[PAIRS + j]
                two = wide[PAIRS + i] * wide[PAIRS + j]
                gram_acc[k] += one[:8] + one[8:]
                gram_acc[half + k] += two[:8] + two[8:]

    folded = jnp.sum(gram_acc[...], axis=1)
    gram_own[0] = lax.dot_general(
        jnp.ones((8, 128), jnp.float32),
        folded,
        (((1,), (1,)), ((), ())),
        precision=lax.Precision.HIGHEST,
        preferred_element_type=jnp.float32,
    )[0:1]
    x_all[core, 0] = tiles[z]

    @pl.loop(1, VN)
    def _(r):
        remote(
            gram_own.at[0], gram_plane.at[VN - 1 - r], gram_send, gram_recv, z, lax.rem(v + r, VN)
        ).start()

    leaving.append(lambda: wait_for(gram_plane, gram_send))
    coming["gram"] = lambda: wait_for(gram_plane, gram_recv)
    pl.semaphore_wait(beyond, 2)
    for s in SENDS["pre"]:
        send_dosage(s)

    def spread(first, count, g):
        @pl.loop(1, VN // 2)
        def _(r):
            block = r_all.at[pl.ds(first, count), mine]
            remote(block, block, res_send.at[1], res_recv.at[4 + g], z, lax.rem(v + 2 * r, VN)).start()

    def residuals_here(first, count, g):
        @pl.when(owner)
        def _():
            wait_for(r_all.at[pl.ds(first, count), pl.ds(0, UNITS - 1)], res_recv.at[4 + g])

        @pl.when(jnp.logical_not(owner))
        def _():
            wait_for(r_all.at[pl.ds(first, count)], res_recv.at[4 + g])

    def line_here(g):
        first, count = GROUPS[g]
        skip = 1 if g == 0 else 0

        @pl.when(owner)
        def _():
            wait_for(r_all.at[pl.ds(first + skip, count - skip), mine], res_recv.at[g])

    def when_owner(what):
        @pl.when(owner)
        def _():
            what()

    take("part")

    @pl.when(owner)
    def _():
        rows = pl.ds(pl.multiple_of(mine * 16, 16), 16)
        lane = lax.broadcasted_iota(jnp.int32, (16, 128), 1)
        word_at = jnp.right_shift(lane, 4) + 8 * core
        words = mask_rows[rows, :].astype(jnp.int32)
        word = jnp.zeros((16, 128), jnp.int32)
        for w in range(16):
            word = jnp.where(word_at == w, jnp.broadcast_to(words[:, w : w + 1], (16, 128)), word)
        observed = jnp.bitwise_and(jnp.right_shift(word, jnp.bitwise_and(lane, 15)), 1).astype(jnp.float32)
        wanted = target[rows, lanes].astype(jnp.float32)
        margin = (row_sum(partial_in[...]) + part[mine, core]) * scale
        r_all[0, mine] = (observed * (margin - wanted)).astype(jnp.bfloat16)
        for s in range(1, ZN):
            remote(r_all.at[0, mine], r_all.at[s, mine], res_send.at[0], res_recv.at[s // 4], at_z(s), v).start()
        spread(0, 1, 0)

    leaving.append(lambda: when_owner(lambda: wait_for(r_all.at[pl.ds(1, ZN - 1), 0], res_send.at[0])))
    leaving.append(lambda: when_owner(lambda: wait_for(r_all.at[pl.ds(1, ZN - 1), 0], res_send.at[1])))
    for g in range(4):
        coming["line%d" % g] = functools.partial(line_here, g)
    coming["res0"] = lambda: residuals_here(0, 1, 0)

    take("gram")
    gram_own[1] = row_sum(gram_plane[...]) + gram_own[0]
    for s in range(1, ZN):
        remote(gram_own.at[1], gram_line.at[s - 1], line_send.at[0], line_recv.at[0], at_z(s), v).start()
    leaving.append(lambda: wait_for(gram_line, line_send.at[0]))
    coming["gram_line"] = lambda: wait_for(gram_line, line_recv.at[0])
    for s in SENDS["post"]:
        send_dosage(s)

    def swap(g):
        first, count = GROUPS[g]
        take("dose%d" % g)
        block = x_all.at[core, pl.ds(first, count)]
        remote(block, block, swap_send, swap_recv.at[g], z, mate).start()
        leaving.append(lambda: wait_for(x_all.at[0, pl.ds(first, count)], swap_send))
        coming["swap%d" % g] = lambda: wait_for(x_all.at[other, pl.ds(first, count)], swap_recv.at[g])

    def pass_on(g):
        first, count = GROUPS[g]
        skip = 1 if g == 0 else 0
        take("line%d" % g)
        when_owner(lambda: spread(first + skip, count - skip, g + 1))
        for _ in range(count - skip):
            leaving.append(lambda: when_owner(lambda: wait_for(r_all.at[pl.ds(1, ZN - 1), 0], res_send.at[1])))
        coming["res%d" % (g + 1)] = lambda: residuals_here(first + skip, count - skip, g + 1)
        for s in SENDS[g]:
            send_dosage(s)

    def turn(g):
        first, count = GROUPS[g]
        take("swap%d" % g)
        for c in range(2):
            x_turned[c, g] = x_all[c, first : first + count].reshape(count * 96, 128).T

    def multiply(g):
        first, count = GROUPS[g]
        if g == 0:
            take("res0")
        take("res%d" % (g + 1))
        rows = jnp.concatenate(
            [
                r_all[first : first + count, 0:6].reshape(count * 96, 128),
                r_all[first : first + count, 6:12].reshape(count * 96, 128),
            ],
            axis=1,
        )
        for c in range(2):
            total = jnp.dot(x_turned[c, g], rows, preferred_element_type=jnp.float32)
            g_acc[c] = total if g == 0 else g_acc[c] + total

    for g in range(4):
        pass_on(g)
    take("gram_line")
    scaling, rows = weight_rows(row_sum(gram_line[...]) + gram_own[1])
    gamma[...] = scaling
    for i in range(2 * PAIRS):
        weights[i : i + 1, :] = rows[i]
    for g in ORDER:
        swap(g)
    for g in ORDER:
        turn(g)
    for g in range(4):
        multiply(g)

    for c in range(2):
        total = g_acc[c]
        g_half[c] = (total[:64, :128] + total[64:, 128:]) * scale
    g_copy = remote(g_half.at[other], g_own.at[core], g_send, g_recv, z, mate)
    g_copy.start()
    leaving.append(g_copy.wait_send)
    coming["g"] = g_copy.wait_recv
    g_own[core] = g_half[core]

    near, far = g_half[core], g_half[other]
    take("hist")
    sub = lax.broadcasted_iota(jnp.int32, (16, 128), 0)
    lane = lax.broadcasted_iota(jnp.int32, (16, 128), 1)
    folds = []
    for i in range(2 * PAIRS):
        both = hist[i, :, lanes].astype(jnp.float32) * near + hist_other[i].astype(jnp.float32) * far
        folds.append(jnp.sum(both, axis=0, keepdims=True))
    sums = jnp.sum(jnp.concatenate(folds, axis=0), axis=1, keepdims=True)
    dots_own[0] = jnp.sum(jnp.where(sub == lane, sums, 0.0), axis=0, keepdims=True)
    for s in range(1, ZN):
        remote(dots_own.at[0], dots_line.at[s - 1], line_send.at[1], line_recv.at[1], at_z(s), v).start()
    leaving.append(lambda: wait_for(dots_line, line_send.at[1]))
    coming["dots_line"] = lambda: wait_for(dots_line, line_recv.at[1])

    take("g")

    take("dots_line")
    dots_mid[0] = row_sum(dots_line[...]) + dots_own[0]

    @pl.loop(1, VN)
    def _(r):
        remote(
            dots_mid.at[0], dots_plane.at[VN - 1 - r], dots_send, dots_recv, z, lax.rem(v + r, VN)
        ).start()

    leaving.append(lambda: wait_for(dots_plane, dots_send))
    coming["dots"] = lambda: wait_for(dots_plane, dots_recv)

    own_rows = pl.ds(pl.multiple_of(z * 64, 64), 64)
    start = coef[own_rows, :].astype(jnp.float32)
    gradient = jnp.concatenate([g_own[0], g_own[1]], axis=1)
    start = start - STEP * (gamma[0:1, 0:1] * gradient)
    limit = STEP * penalty_ref[...]

    take("dots")
    dots = row_sum(dots_plane[...]) + dots_mid[0]
    mix = jnp.sum(weights[...] * dots, axis=1, keepdims=True)
    along = mix[0:1] * hist[0].astype(jnp.float32)
    for i in range(1, 2 * PAIRS):
        along = along + mix[i : i + 1] * hist[i].astype(jnp.float32)
    moved = start - STEP * along
    out_ref[...] = moved - jnp.clip(moved, -limit, limit)
    finish()


def per_device(dosage, coefficients, targets, mask_words, penalty, past_steps, past_changes):
    samples, variants = dosage.shape
    traits = coefficients.shape[1]
    owned = variants // ZN
    f32, bf16 = jnp.float32, jnp.bfloat16
    vmem = pltpu.VMEM
    dma = pltpu.SemaphoreType.DMA
    anywhere = pl.BlockSpec(memory_space=pl.ANY)
    return pl.pallas_call(
        kernel,
        out_shape=jax.ShapeDtypeStruct((owned, traits), f32),
        in_specs=[anywhere] * 4 + [pl.BlockSpec(memory_space=vmem)] + [anywhere] * 2,
        out_specs=pl.BlockSpec(memory_space=vmem),
        scratch_shapes=[
            vmem((samples, variants), bf16),
            vmem((variants, traits), bf16),
            vmem((samples, traits), bf16),
            vmem(mask_words.shape[::-1], jnp.int32),
            vmem(mask_words.shape, f32),
            vmem((2 * PAIRS, owned, traits), bf16),
            vmem((UNITS, 2, 16, 128), f32),
            vmem((ZN, 96, 128), bf16),
            vmem((2, ZN, 96, 128), bf16),
            vmem((2, 4, 128, 384), bf16),
            vmem((ZN, UNITS, 16, 128), bf16),
            vmem((VN - 1, 16, 128), f32),
            vmem((2 * PAIRS, owned, 128), bf16),
            vmem((128, 8, 128), f32),
            vmem((2, 1, 128), f32),
            vmem((VN - 1, 1, 128), f32),
            vmem((ZN - 1, 1, 128), f32),
            vmem((2 * PAIRS, 128), f32),
            vmem((1, 128), f32),
            vmem((2, 128, 256), f32),
            vmem((2, owned, 128), f32),
            vmem((2, owned, 128), f32),
            vmem((1, 1, 128), f32),
            vmem((ZN - 1, 1, 128), f32),
            vmem((1, 1, 128), f32),
            vmem((VN - 1, 1, 128), f32),
            dma((6,)),
            dma,
            dma,
            dma,
            dma((4,)),
            dma,
            dma((4,)),
            dma,
            dma,
            dma,
            dma,
            dma((2,)),
            dma((2,)),
            dma((2,)),
            dma((9,)),
            dma,
            dma,
            dma,
            dma,
            pltpu.SemaphoreType.REGULAR,
        ],
        compiler_params=pltpu.CompilerParams(
            collective_id=0, has_side_effects=True, vmem_limit_bytes=60 * 1024 * 1024
        ),
    )(dosage, coefficients, targets, mask_words.T, penalty[None, :], past_steps, past_changes)


def solution(mesh):
    in_specs = (
        P("samp", "var"),
        P("var", None),
        P("samp", None),
        P("samp", None),
        P(),
        P(None, ("var", "samp"), None),
        P(None, ("var", "samp"), None),
    )
    out_specs = P(("var", "samp"), None)
    return jax.shard_map(
        per_device, mesh=mesh, in_specs=in_specs, out_specs=out_specs, check_vma=False
    )
```

```python
import functools

import jax
import jax.numpy as jnp
from jax import lax
from jax.experimental import pallas as pl
from jax.experimental.pallas import tpu as pltpu
from jax.sharding import PartitionSpec as P

MESH = pl.DeviceIdType.MESH
STEP = 0.5
ZN = 16
VN = 32
PAIRS = 8
UNITS = 12
OFFSET = [0] + [(s + 1) // 2 if s % 2 else -(s // 2) for s in range(1, ZN)]
GROUPS = [(0, 4), (4, 4), (8, 4), (12, 4)]
SENDS = {"near": (8, 7, 6, 5, 4, 3, 2, 1), "pre": (15,), "post": (), 0: (14, 13), 1: (12, 11, 10, 9), 2: (), 3: ()}
ORDER = (0, 1, 3, 2)


def wait_for(ref, sem):
    pltpu.make_async_copy(ref, ref, sem).wait()


def row_sum(block):
    return jnp.sum(block, axis=0)


def pair_index(i, j):
    return i * PAIRS - (i * (i - 1)) // 2 + (j - i)


def weight_rows(sums):
    lane = lax.broadcasted_iota(jnp.int32, (1, 128), 1)

    def entry(k):
        return jnp.broadcast_to(sums[:, k : k + 1], (1, 128))

    def unit(k):
        return jnp.where(lane == k, 1.0, 0.0)

    half = PAIRS * (PAIRS + 1) // 2
    upper = {(i, j): entry(pair_index(i, j)) for i in range(PAIRS) for j in range(i, PAIRS)}
    gram = {(i, j): entry(half + pair_index(i, j)) for i in range(PAIRS) for j in range(i, PAIRS)}
    scaling = upper[PAIRS - 1, PAIRS - 1] / gram[PAIRS - 1, PAIRS - 1]
    inner = [None] * PAIRS
    for i in reversed(range(PAIRS)):
        total = unit(i)
        for j in range(i + 1, PAIRS):
            total = total - upper[i, j] * inner[j]
        inner[i] = total / upper[i, i]
    outer = [None] * PAIRS
    for i in range(PAIRS):
        total = gram[min(i, 0), max(i, 0)] * inner[0]
        for j in range(1, PAIRS):
            total = total + gram[min(i, j), max(i, j)] * inner[j]
        total = upper[i, i] * inner[i] + scaling * total - scaling * unit(PAIRS + i)
        for j in range(i):
            total = total - upper[j, i] * outer[j]
        outer[i] = total / upper[i, i]
    return scaling, outer + [-scaling * row for row in inner]


def kernel(
    dosage_hbm,
    coef_hbm,
    target_hbm,
    mask_hbm,
    penalty_ref,
    steps_hbm,
    changes_hbm,
    out_ref,
    dosage,
    coef,
    target,
    mask,
    mask_rows,
    hist,
    part,
    tiles,
    x_all,
    x_turned,
    r_all,
    partial_in,
    hist_other,
    gram_acc,
    gram_own,
    gram_plane,
    gram_line,
    weights,
    gamma,
    g_acc,
    g_half,
    g_own,
    dots_own,
    dots_line,
    dots_mid,
    dots_plane,
    local_sem,
    part_send,
    part_recv,
    dose_send,
    dose_recv,
    swap_send,
    swap_recv,
    hist_send,
    hist_recv,
    gram_send,
    gram_recv,
    line_send,
    line_recv,
    res_send,
    res_recv,
    g_send,
    g_recv,
    dots_send,
    dots_recv,
    beyond,
):
    z = lax.axis_index("samp")
    v = lax.axis_index("var")
    core = lax.rem(v, 2)
    chip = lax.div(v, 2)
    other = 1 - core
    mate = v + 1 - 2 * core
    scale = (VN * dosage.shape[1]) ** -0.5

    def unit_of(c):
        x, y = lax.div(c, 4), lax.rem(c, 4)
        s = lax.rem(x + y, 4)
        return s < 3, 3 * x + jnp.minimum(s, 2)

    owner, mine = unit_of(chip)
    lanes = pl.ds(pl.multiple_of(core * 128, 128), 128)
    other_lanes = pl.ds(pl.multiple_of(other * 128, 128), 128)

    def at_z(s):
        return lax.rem(z - OFFSET[s] + ZN, ZN)

    def remote(src, dst, send, recv, zz, vv):
        return pltpu.make_async_remote_copy(
            src_ref=src, dst_ref=dst, send_sem=send, recv_sem=recv, device_id=(zz, vv), device_id_type=MESH
        )

    coming, leaving = {}, []

    def take(name):
        coming.pop(name)()

    def finish():
        for name in list(coming):
            take(name)
        for left in leaving:
            left()

    barrier = pltpu.get_barrier_semaphore()

    for r in (4, 12, 3, 13, 2, 14, 1, 15):
        pl.semaphore_signal(barrier, inc=1, device_id=(lax.rem(z + r, ZN), v), device_id_type=MESH)

    @pl.loop(1, VN)
    def _(r):
        pl.semaphore_signal(barrier, inc=1, device_id=(z, lax.rem(v + r, VN)), device_id_type=MESH)

    loads = [
        pltpu.make_async_copy(dosage_hbm, dosage, local_sem.at[0]),
        pltpu.make_async_copy(coef_hbm, coef, local_sem.at[1]),
        pltpu.make_async_copy(steps_hbm, hist.at[pl.ds(0, PAIRS)], local_sem.at[2]),
        pltpu.make_async_copy(changes_hbm, hist.at[pl.ds(PAIRS, PAIRS)], local_sem.at[3]),
        pltpu.make_async_copy(target_hbm, target, local_sem.at[4]),
        pltpu.make_async_copy(mask_hbm, mask, local_sem.at[5]),
    ]
    for load in loads:
        load.start()

    loads[0].wait()
    loads[1].wait()
    product = jnp.dot(dosage[...], coef[...], preferred_element_type=jnp.float32)
    for u in range(UNITS):
        for h in range(2):
            part[u, h] = product[16 * u : 16 * u + 16, 128 * h : 128 * h + 128]
    for j in range(ZN // 2):
        top = dosage[0:96, 128 * j : 128 * j + 128]
        low = dosage[96:192, 128 * j : 128 * j + 128]
        tiles[2 * j] = jnp.concatenate([top[:, :64], low[:, :64]], axis=1)
        tiles[2 * j + 1] = jnp.concatenate([top[:, 64:], low[:, 64:]], axis=1)
    for load in loads[2:]:
        load.wait()
    mask_rows[...] = mask[...].astype(jnp.float32).T

    pl.semaphore_wait(barrier, VN - 1 + 8)
    for r in (4, 12):
        pl.semaphore_signal(beyond, inc=1, device_id=(lax.rem(z + r, ZN), v), device_id_type=MESH)

    for u in range(UNITS):
        x, y = u // 3, (u % 3 - u // 3) % 4
        for h in range(2):
            dest = 2 * (4 * x + y) + h

            @pl.when(v != dest)
            def _():
                place = lax.rem(v - dest + VN, VN) - 1
                remote(part.at[u, h], partial_in.at[place], part_send, part_recv, z, dest).start()

    def part_left():
        @pl.when(owner)
        def _():
            wait_for(part.at[pl.ds(0, UNITS - 1)], part_send)
            wait_for(part.at[0, 0], part_send)

        @pl.when(jnp.logical_not(owner))
        def _():
            wait_for(part, part_send)

    def part_here():
        @pl.when(owner)
        def _():
            wait_for(partial_in, part_recv)

    leaving.append(part_left)
    coming["part"] = part_here

    def send_dosage(s):
        g = s // 4
        remote(tiles.at[at_z(s)], x_all.at[core, s], dose_send, dose_recv.at[g], at_z(s), v).start()
        leaving.append(lambda: wait_for(tiles.at[0], dose_send))

    def dosage_here(g):
        first, count = GROUPS[g]
        skip = 1 if g == 0 else 0
        wait_for(x_all.at[core, pl.ds(first + skip, count - skip)], dose_recv.at[g])

    for s in SENDS["near"]:
        send_dosage(s)
    for g in range(4):
        coming["dose%d" % g] = functools.partial(dosage_here, g)
    hist_copy = remote(hist.at[:, :, other_lanes], hist_other, hist_send, hist_recv, z, mate)
    hist_copy.start()
    leaving.append(hist_copy.wait_send)
    coming["hist"] = hist_copy.wait_recv

    gram_acc[...] = jnp.zeros_like(gram_acc)
    half = PAIRS * (PAIRS + 1) // 2

    @pl.loop(0, 8)
    def _(t):
        rows = pl.ds(pl.multiple_of(lax.div(t, 2) * 16, 16), 16)
        cols = pl.ds(pl.multiple_of(lax.rem(t, 2) * 128, 128), 128)
        wide = [hist[i, rows, cols].astype(jnp.float32) for i in range(2 * PAIRS)]
        for i in range(PAIRS):
            for j in range(i, PAIRS):
                k = pair_index(i, j)
                one = wide[i] * wide[PAIRS + j]
                two = wide[PAIRS + i] * wide[PAIRS + j]
                gram_acc[k] += one[:8] + one[8:]
                gram_acc[half + k] += two[:8] + two[8:]

    folded = jnp.sum(gram_acc[...], axis=1)
    gram_own[0] = lax.dot_general(
        jnp.ones((8, 128), jnp.float32),
        folded,
        (((1,), (1,)), ((), ())),
        precision=lax.Precision.HIGHEST,
        preferred_element_type=jnp.float32,
    )[0:1]
    x_all[core, 0] = tiles[z]

    @pl.loop(1, VN)
    def _(r):
        remote(
            gram_own.at[0], gram_plane.at[VN - 1 - r], gram_send, gram_recv, z, lax.rem(v + r, VN)
        ).start()

    leaving.append(lambda: wait_for(gram_plane, gram_send))
    coming["gram"] = lambda: wait_for(gram_plane, gram_recv)
    pl.semaphore_wait(beyond, 2)
    for s in SENDS["pre"]:
        send_dosage(s)

    def spread(first, count, g):
        @pl.loop(1, VN // 2)
        def _(r):
            block = r_all.at[pl.ds(first, count), mine]
            remote(block, block, res_send.at[1], res_recv.at[4 + g], z, lax.rem(v + 2 * r, VN)).start()

    def residuals_here(first, count, g):
        @pl.when(owner)
        def _():
            wait_for(r_all.at[pl.ds(first, count), pl.ds(0, UNITS - 1)], res_recv.at[4 + g])

        @pl.when(jnp.logical_not(owner))
        def _():
            wait_for(r_all.at[pl.ds(first, count)], res_recv.at[4 + g])

    def line_here(g):
        first, count = GROUPS[g]
        skip = 1 if g == 0 else 0

        @pl.when(owner)
        def _():
            wait_for(r_all.at[pl.ds(first + skip, count - skip), mine], res_recv.at[g])

    def when_owner(what):
        @pl.when(owner)
        def _():
            what()

    take("part")

    @pl.when(owner)
    def _():
        rows = pl.ds(pl.multiple_of(mine * 16, 16), 16)
        lane = lax.broadcasted_iota(jnp.int32, (16, 128), 1)
        word_at = jnp.right_shift(lane, 4) + 8 * core
        words = mask_rows[rows, :].astype(jnp.int32)
        word = jnp.zeros((16, 128), jnp.int32)
        for w in range(16):
            word = jnp.where(word_at == w, jnp.broadcast_to(words[:, w : w + 1], (16, 128)), word)
        observed = jnp.bitwise_and(jnp.right_shift(word, jnp.bitwise_and(lane, 15)), 1).astype(jnp.float32)
        wanted = target[rows, lanes].astype(jnp.float32)
        margin = (row_sum(partial_in[...]) + part[mine, core]) * scale
        r_all[0, mine] = (observed * (margin - wanted)).astype(jnp.bfloat16)
        for s in range(1, ZN):
            remote(r_all.at[0, mine], r_all.at[s, mine], res_send.at[0], res_recv.at[s // 4], at_z(s), v).start()
        spread(0, 1, 0)

    leaving.append(lambda: when_owner(lambda: wait_for(r_all.at[pl.ds(1, ZN - 1), 0], res_send.at[0])))
    leaving.append(lambda: when_owner(lambda: wait_for(r_all.at[pl.ds(1, ZN - 1), 0], res_send.at[1])))
    for g in range(4):
        coming["line%d" % g] = functools.partial(line_here, g)
    coming["res0"] = lambda: residuals_here(0, 1, 0)

    take("gram")
    gram_own[1] = row_sum(gram_plane[...]) + gram_own[0]
    for s in range(1, ZN):
        remote(gram_own.at[1], gram_line.at[s - 1], line_send.at[0], line_recv.at[0], at_z(s), v).start()
    leaving.append(lambda: wait_for(gram_line, line_send.at[0]))
    coming["gram_line"] = lambda: wait_for(gram_line, line_recv.at[0])
    for s in SENDS["post"]:
        send_dosage(s)

    def swap(g):
        first, count = GROUPS[g]
        take("dose%d" % g)
        block = x_all.at[core, pl.ds(first, count)]
        remote(block, block, swap_send, swap_recv.at[g], z, mate).start()
        leaving.append(lambda: wait_for(x_all.at[0, pl.ds(first, count)], swap_send))
        coming["swap%d" % g] = lambda: wait_for(x_all.at[other, pl.ds(first, count)], swap_recv.at[g])

    def pass_on(g):
        first, count = GROUPS[g]
        skip = 1 if g == 0 else 0
        take("line%d" % g)
        when_owner(lambda: spread(first + skip, count - skip, g + 1))
        for _ in range(count - skip):
            leaving.append(lambda: when_owner(lambda: wait_for(r_all.at[pl.ds(1, ZN - 1), 0], res_send.at[1])))
        coming["res%d" % (g + 1)] = lambda: residuals_here(first + skip, count - skip, g + 1)
        for s in SENDS[g]:
            send_dosage(s)

    def turn(g):
        first, count = GROUPS[g]
        take("swap%d" % g)
        for c in range(2):
            x_turned[c, g] = x_all[c, first : first + count].reshape(count * 96, 128).T

    def multiply(g):
        first, count = GROUPS[g]
        if g == 0:
            take("res0")
        take("res%d" % (g + 1))
        rows = jnp.concatenate(
            [
                r_all[first : first + count, 0:6].reshape(count * 96, 128),
                r_all[first : first + count, 6:12].reshape(count * 96, 128),
            ],
            axis=1,
        )
        for c in range(2):
            total = jnp.dot(x_turned[c, g], rows, preferred_element_type=jnp.float32)
            g_acc[c] = total if g == 0 else g_acc[c] + total

    for g in range(4):
        pass_on(g)
    take("gram_line")
    scaling, rows = weight_rows(row_sum(gram_line[...]) + gram_own[1])
    gamma[...] = scaling
    for i in range(2 * PAIRS):
        weights[i : i + 1, :] = rows[i]
    for g in ORDER:
        swap(g)
    for g in ORDER:
        turn(g)
    for g in range(4):
        multiply(g)

    for c in range(2):
        total = g_acc[c]
        g_half[c] = (total[:64, :128] + total[64:, 128:]) * scale
    g_copy = remote(g_half.at[other], g_own.at[core], g_send, g_recv, z, mate)
    g_copy.start()
    leaving.append(g_copy.wait_send)
    coming["g"] = g_copy.wait_recv
    g_own[core] = g_half[core]

    near, far = g_half[core], g_half[other]
    take("hist")
    sub = lax.broadcasted_iota(jnp.int32, (16, 128), 0)
    lane = lax.broadcasted_iota(jnp.int32, (16, 128), 1)
    folds = []
    for i in range(2 * PAIRS):
        both = hist[i, :, lanes].astype(jnp.float32) * near + hist_other[i].astype(jnp.float32) * far
        folds.append(jnp.sum(both, axis=0, keepdims=True))
    sums = jnp.sum(jnp.concatenate(folds, axis=0), axis=1, keepdims=True)
    dots_own[0] = jnp.sum(jnp.where(sub == lane, sums, 0.0), axis=0, keepdims=True)
    for s in range(1, ZN):
        remote(dots_own.at[0], dots_line.at[s - 1], line_send.at[1], line_recv.at[1], at_z(s), v).start()
    leaving.append(lambda: wait_for(dots_line, line_send.at[1]))
    coming["dots_line"] = lambda: wait_for(dots_line, line_recv.at[1])

    take("g")

    take("dots_line")
    dots_mid[0] = row_sum(dots_line[...]) + dots_own[0]

    @pl.loop(1, VN)
    def _(r):
        remote(
            dots_mid.at[0], dots_plane.at[VN - 1 - r], dots_send, dots_recv, z, lax.rem(v + r, VN)
        ).start()

    leaving.append(lambda: wait_for(dots_plane, dots_send))
    coming["dots"] = lambda: wait_for(dots_plane, dots_recv)

    own_rows = pl.ds(pl.multiple_of(z * 64, 64), 64)
    start = coef[own_rows, :].astype(jnp.float32)
    gradient = jnp.concatenate([g_own[0], g_own[1]], axis=1)
    start = start - STEP * (gamma[0:1, 0:1] * gradient)
    limit = STEP * penalty_ref[...]

    take("dots")
    dots = row_sum(dots_plane[...]) + dots_mid[0]
    mix = jnp.sum(weights[...] * dots, axis=1, keepdims=True)
    along = mix[0:1] * hist[0].astype(jnp.float32)
    for i in range(1, 2 * PAIRS):
        along = along + mix[i : i + 1] * hist[i].astype(jnp.float32)
    moved = start - STEP * along
    out_ref[...] = moved - jnp.clip(moved, -limit, limit)
    finish()


def per_device(dosage, coefficients, targets, mask_words, penalty, past_steps, past_changes):
    samples, variants = dosage.shape
    traits = coefficients.shape[1]
    owned = variants // ZN
    f32, bf16 = jnp.float32, jnp.bfloat16
    vmem = pltpu.VMEM
    dma = pltpu.SemaphoreType.DMA
    anywhere = pl.BlockSpec(memory_space=pl.ANY)
    return pl.pallas_call(
        kernel,
        out_shape=jax.ShapeDtypeStruct((owned, traits), f32),
        in_specs=[anywhere] * 4 + [pl.BlockSpec(memory_space=vmem)] + [anywhere] * 2,
        out_specs=pl.BlockSpec(memory_space=vmem),
        scratch_shapes=[
            vmem((samples, variants), bf16),
            vmem((variants, traits), bf16),
            vmem((samples, traits), bf16),
            vmem(mask_words.shape[::-1], jnp.int32),
            vmem(mask_words.shape, f32),
            vmem((2 * PAIRS, owned, traits), bf16),
            vmem((UNITS, 2, 16, 128), f32),
            vmem((ZN, 96, 128), bf16),
            vmem((2, ZN, 96, 128), bf16),
            vmem((2, 4, 128, 384), bf16),
            vmem((ZN, UNITS, 16, 128), bf16),
            vmem((VN - 1, 16, 128), f32),
            vmem((2 * PAIRS, owned, 128), bf16),
            vmem((128, 8, 128), f32),
            vmem((2, 1, 128), f32),
            vmem((VN - 1, 1, 128), f32),
            vmem((ZN - 1, 1, 128), f32),
            vmem((2 * PAIRS, 128), f32),
            vmem((1, 128), f32),
            vmem((2, 128, 256), f32),
            vmem((2, owned, 128), f32),
            vmem((2, owned, 128), f32),
            vmem((1, 1, 128), f32),
            vmem((ZN - 1, 1, 128), f32),
            vmem((1, 1, 128), f32),
            vmem((VN - 1, 1, 128), f32),
            dma((6,)),
            dma,
            dma,
            dma,
            dma((4,)),
            dma,
            dma((4,)),
            dma,
            dma,
            dma,
            dma,
            dma((2,)),
            dma((2,)),
            dma((2,)),
            dma((9,)),
            dma,
            dma,
            dma,
            dma,
            pltpu.SemaphoreType.REGULAR,
        ],
        compiler_params=pltpu.CompilerParams(
            collective_id=0, has_side_effects=True, vmem_limit_bytes=55130 * 1024
        ),
    )(dosage, coefficients, targets, mask_words.T, penalty[None, :], past_steps, past_changes)


def solution(mesh):
    in_specs = (
        P("samp", "var"),
        P("var", None),
        P("samp", None),
        P("samp", None),
        P(),
        P(None, ("var", "samp"), None),
        P(None, ("var", "samp"), None),
    )
    out_specs = P(("var", "samp"), None)
    return jax.shard_map(
        per_device, mesh=mesh, in_specs=in_specs, out_specs=out_specs, check_vma=False
    )
```

```python
import functools

import jax
import jax.numpy as jnp
from jax import lax
from jax.experimental import pallas as pl
from jax.experimental.pallas import tpu as pltpu
from jax.sharding import PartitionSpec as P

MESH = pl.DeviceIdType.MESH
STEP = 0.5
ZN = 16
VN = 32
PAIRS = 8
UNITS = 12
OFFSET = [0] + [(s + 1) // 2 if s % 2 else -(s // 2) for s in range(1, ZN)]
GROUPS = [(0, 4), (4, 4), (8, 4), (12, 4)]
SENDS = {"near": (8, 7, 6, 5, 4, 3, 2, 1), "pre": (15,), "post": (), 0: (14, 13), 1: (12, 11, 10, 9), 2: (), 3: ()}
ORDER = (0, 1, 3, 2)


def wait_for(ref, sem):
    pltpu.make_async_copy(ref, ref, sem).wait()


def row_sum(block):
    return jnp.sum(block, axis=0)


def pair_index(i, j):
    return i * PAIRS - (i * (i - 1)) // 2 + (j - i)


def weight_rows(sums):
    lane = lax.broadcasted_iota(jnp.int32, (1, 128), 1)

    def entry(k):
        return jnp.broadcast_to(sums[:, k : k + 1], (1, 128))

    def unit(k):
        return jnp.where(lane == k, 1.0, 0.0)

    half = PAIRS * (PAIRS + 1) // 2
    upper = {(i, j): entry(pair_index(i, j)) for i in range(PAIRS) for j in range(i, PAIRS)}
    gram = {(i, j): entry(half + pair_index(i, j)) for i in range(PAIRS) for j in range(i, PAIRS)}
    scaling = upper[PAIRS - 1, PAIRS - 1] / gram[PAIRS - 1, PAIRS - 1]
    inner = [None] * PAIRS
    for i in reversed(range(PAIRS)):
        total = unit(i)
        for j in range(i + 1, PAIRS):
            total = total - upper[i, j] * inner[j]
        inner[i] = total / upper[i, i]
    outer = [None] * PAIRS
    for i in range(PAIRS):
        total = gram[min(i, 0), max(i, 0)] * inner[0]
        for j in range(1, PAIRS):
            total = total + gram[min(i, j), max(i, j)] * inner[j]
        total = upper[i, i] * inner[i] + scaling * total - scaling * unit(PAIRS + i)
        for j in range(i):
            total = total - upper[j, i] * outer[j]
        outer[i] = total / upper[i, i]
    return scaling, outer + [-scaling * row for row in inner]


def kernel(
    dosage_hbm,
    coef_hbm,
    target_hbm,
    mask_hbm,
    penalty_ref,
    steps_hbm,
    changes_hbm,
    out_ref,
    dosage,
    coef,
    target,
    mask,
    mask_rows,
    hist,
    part,
    tiles,
    x_all,
    x_turned,
    r_all,
    partial_in,
    hist_other,
    gram_acc,
    gram_own,
    gram_plane,
    gram_line,
    weights,
    gamma,
    g_acc,
    g_half,
    g_own,
    dots_own,
    dots_line,
    dots_mid,
    dots_plane,
    local_sem,
    part_send,
    part_recv,
    dose_send,
    dose_recv,
    swap_send,
    swap_recv,
    hist_send,
    hist_recv,
    gram_send,
    gram_recv,
    line_send,
    line_recv,
    res_send,
    res_recv,
    g_send,
    g_recv,
    dots_send,
    dots_recv,
    beyond,
):
    z = lax.axis_index("samp")
    v = lax.axis_index("var")
    core = lax.rem(v, 2)
    chip = lax.div(v, 2)
    other = 1 - core
    mate = v + 1 - 2 * core
    scale = (VN * dosage.shape[1]) ** -0.5

    def unit_of(c):
        x, y = lax.div(c, 4), lax.rem(c, 4)
        s = lax.rem(x + y, 4)
        return s < 3, 3 * x + jnp.minimum(s, 2)

    owner, mine = unit_of(chip)
    lanes = pl.ds(pl.multiple_of(core * 128, 128), 128)
    other_lanes = pl.ds(pl.multiple_of(other * 128, 128), 128)

    def at_z(s):
        return lax.rem(z - OFFSET[s] + ZN, ZN)

    def remote(src, dst, send, recv, zz, vv):
        return pltpu.make_async_remote_copy(
            src_ref=src, dst_ref=dst, send_sem=send, recv_sem=recv, device_id=(zz, vv), device_id_type=MESH
        )

    coming, leaving = {}, []

    def take(name):
        coming.pop(name)()

    def finish():
        for name in list(coming):
            take(name)
        for left in leaving:
            left()

    barrier = pltpu.get_barrier_semaphore()

    for r in (4, 12, 3, 13, 2, 14, 1, 15):
        pl.semaphore_signal(barrier, inc=1, device_id=(lax.rem(z + r, ZN), v), device_id_type=MESH)

    @pl.loop(1, VN)
    def _(r):
        pl.semaphore_signal(barrier, inc=1, device_id=(z, lax.rem(v + r, VN)), device_id_type=MESH)

    loads = [
        pltpu.make_async_copy(dosage_hbm, dosage, local_sem.at[0]),
        pltpu.make_async_copy(coef_hbm, coef, local_sem.at[1]),
        pltpu.make_async_copy(steps_hbm, hist.at[pl.ds(0, PAIRS)], local_sem.at[2]),
        pltpu.make_async_copy(changes_hbm, hist.at[pl.ds(PAIRS, PAIRS)], local_sem.at[3]),
        pltpu.make_async_copy(target_hbm, target, local_sem.at[4]),
        pltpu.make_async_copy(mask_hbm, mask, local_sem.at[5]),
    ]
    for load in loads:
        load.start()

    loads[0].wait()
    loads[1].wait()
    product = jnp.dot(dosage[...], coef[...], preferred_element_type=jnp.float32)
    for u in range(UNITS):
        for h in range(2):
            part[u, h] = product[16 * u : 16 * u + 16, 128 * h : 128 * h + 128]
    for j in range(ZN // 2):
        top = dosage[0:96, 128 * j : 128 * j + 128]
        low = dosage[96:192, 128 * j : 128 * j + 128]
        tiles[2 * j] = jnp.concatenate([top[:, :64], low[:, :64]], axis=1)
        tiles[2 * j + 1] = jnp.concatenate([top[:, 64:], low[:, 64:]], axis=1)
    for load in loads[2:]:
        load.wait()
    mask_rows[...] = mask[...].astype(jnp.float32).T

    pl.semaphore_wait(barrier, VN - 1 + 8)
    for r in (4, 12):
        pl.semaphore_signal(beyond, inc=1, device_id=(lax.rem(z + r, ZN), v), device_id_type=MESH)

    for u in range(UNITS):
        x, y = u // 3, (u % 3 - u // 3) % 4
        for h in range(2):
            dest = 2 * (4 * x + y) + h

            @pl.when(v != dest)
            def _():
                place = lax.rem(v - dest + VN, VN) - 1
                remote(part.at[u, h], partial_in.at[place], part_send, part_recv, z, dest).start()

    def part_left():
        @pl.when(owner)
        def _():
            wait_for(part.at[pl.ds(0, UNITS - 1)], part_send)
            wait_for(part.at[0, 0], part_send)

        @pl.when(jnp.logical_not(owner))
        def _():
            wait_for(part, part_send)

    def part_here():
        @pl.when(owner)
        def _():
            wait_for(partial_in, part_recv)

    leaving.append(part_left)
    coming["part"] = part_here

    def send_dosage(s):
        g = s // 4
        remote(tiles.at[at_z(s)], x_all.at[core, s], dose_send, dose_recv.at[g], at_z(s), v).start()
        leaving.append(lambda: wait_for(tiles.at[0], dose_send))

    def dosage_here(g):
        first, count = GROUPS[g]
        skip = 1 if g == 0 else 0
        wait_for(x_all.at[core, pl.ds(first + skip, count - skip)], dose_recv.at[g])

    for s in SENDS["near"]:
        send_dosage(s)
    for g in range(4):
        coming["dose%d" % g] = functools.partial(dosage_here, g)
    hist_copy = remote(hist.at[:, :, other_lanes], hist_other, hist_send, hist_recv, z, mate)
    hist_copy.start()
    leaving.append(hist_copy.wait_send)
    coming["hist"] = hist_copy.wait_recv

    gram_acc[...] = jnp.zeros_like(gram_acc)
    half = PAIRS * (PAIRS + 1) // 2

    @pl.loop(0, 8)
    def _(t):
        rows = pl.ds(pl.multiple_of(lax.div(t, 2) * 16, 16), 16)
        cols = pl.ds(pl.multiple_of(lax.rem(t, 2) * 128, 128), 128)
        wide = [hist[i, rows, cols].astype(jnp.float32) for i in range(2 * PAIRS)]
        for i in range(PAIRS):
            for j in range(i, PAIRS):
                k = pair_index(i, j)
                one = wide[i] * wide[PAIRS + j]
                two = wide[PAIRS + i] * wide[PAIRS + j]
                gram_acc[k] += one[:8] + one[8:]
                gram_acc[half + k] += two[:8] + two[8:]

    folded = jnp.sum(gram_acc[...], axis=1)
    gram_own[0] = lax.dot_general(
        jnp.ones((8, 128), jnp.float32),
        folded,
        (((1,), (1,)), ((), ())),
        precision=lax.Precision.HIGHEST,
        preferred_element_type=jnp.float32,
    )[0:1]
    x_all[core, 0] = tiles[z]

    pl.semaphore_wait(beyond, 2)
    for s in SENDS["pre"]:
        send_dosage(s)

    def spread(first, count, g):
        @pl.loop(1, VN // 2)
        def _(r):
            block = r_all.at[pl.ds(first, count), mine]
            remote(block, block, res_send.at[1], res_recv.at[4 + g], z, lax.rem(v + 2 * r, VN)).start()

    def residuals_here(first, count, g):
        @pl.when(owner)
        def _():
            wait_for(r_all.at[pl.ds(first, count), pl.ds(0, UNITS - 1)], res_recv.at[4 + g])

        @pl.when(jnp.logical_not(owner))
        def _():
            wait_for(r_all.at[pl.ds(first, count)], res_recv.at[4 + g])

    def line_here(g):
        first, count = GROUPS[g]
        skip = 1 if g == 0 else 0

        @pl.when(owner)
        def _():
            wait_for(r_all.at[pl.ds(first + skip, count - skip), mine], res_recv.at[g])

    def when_owner(what):
        @pl.when(owner)
        def _():
            what()

    take("part")

    @pl.when(owner)
    def _():
        rows = pl.ds(pl.multiple_of(mine * 16, 16), 16)
        lane = lax.broadcasted_iota(jnp.int32, (16, 128), 1)
        word_at = jnp.right_shift(lane, 4) + 8 * core
        words = mask_rows[rows, :].astype(jnp.int32)
        word = jnp.zeros((16, 128), jnp.int32)
        for w in range(16):
            word = jnp.where(word_at == w, jnp.broadcast_to(words[:, w : w + 1], (16, 128)), word)
        observed = jnp.bitwise_and(jnp.right_shift(word, jnp.bitwise_and(lane, 15)), 1).astype(jnp.float32)
        wanted = target[rows, lanes].astype(jnp.float32)
        margin = (row_sum(partial_in[...]) + part[mine, core]) * scale
        r_all[0, mine] = (observed * (margin - wanted)).astype(jnp.bfloat16)
        for s in range(1, ZN):
            remote(r_all.at[0, mine], r_all.at[s, mine], res_send.at[0], res_recv.at[s // 4], at_z(s), v).start()
        spread(0, 1, 0)

    leaving.append(lambda: when_owner(lambda: wait_for(r_all.at[pl.ds(1, ZN - 1), 0], res_send.at[0])))
    leaving.append(lambda: when_owner(lambda: wait_for(r_all.at[pl.ds(1, ZN - 1), 0], res_send.at[1])))
    for g in range(4):
        coming["line%d" % g] = functools.partial(line_here, g)
    coming["res0"] = lambda: residuals_here(0, 1, 0)

    @pl.loop(1, VN)
    def _(r):
        remote(
            gram_own.at[0], gram_plane.at[VN - 1 - r], gram_send, gram_recv, z, lax.rem(v + r, VN)
        ).start()

    leaving.append(lambda: wait_for(gram_plane, gram_send))
    coming["gram"] = lambda: wait_for(gram_plane, gram_recv)

    def swap(g):
        first, count = GROUPS[g]
        take("dose%d" % g)
        block = x_all.at[core, pl.ds(first, count)]
        remote(block, block, swap_send, swap_recv.at[g], z, mate).start()
        leaving.append(lambda: wait_for(x_all.at[0, pl.ds(first, count)], swap_send))
        coming["swap%d" % g] = lambda: wait_for(x_all.at[other, pl.ds(first, count)], swap_recv.at[g])

    def pass_on(g):
        first, count = GROUPS[g]
        skip = 1 if g == 0 else 0
        take("line%d" % g)
        when_owner(lambda: spread(first + skip, count - skip, g + 1))
        for _ in range(count - skip):
            leaving.append(lambda: when_owner(lambda: wait_for(r_all.at[pl.ds(1, ZN - 1), 0], res_send.at[1])))
        coming["res%d" % (g + 1)] = lambda: residuals_here(first + skip, count - skip, g + 1)
        for s in SENDS[g]:
            send_dosage(s)

    def turn(g):
        first, count = GROUPS[g]
        take("swap%d" % g)
        for c in range(2):
            x_turned[c, g] = x_all[c, first : first + count].reshape(count * 96, 128).T

    def multiply(g):
        first, count = GROUPS[g]
        if g == 0:
            take("res0")
        take("res%d" % (g + 1))
        rows = jnp.concatenate(
            [
                r_all[first : first + count, 0:6].reshape(count * 96, 128),
                r_all[first : first + count, 6:12].reshape(count * 96, 128),
            ],
            axis=1,
        )
        for c in range(2):
            total = jnp.dot(x_turned[c, g], rows, preferred_element_type=jnp.float32)
            g_acc[c] = total if g == 0 else g_acc[c] + total

    for g in range(4):
        pass_on(g)
    take("gram")
    gram_own[1] = row_sum(gram_plane[...]) + gram_own[0]
    for s in range(1, ZN):
        remote(gram_own.at[1], gram_line.at[s - 1], line_send.at[0], line_recv.at[0], at_z(s), v).start()
    leaving.append(lambda: wait_for(gram_line, line_send.at[0]))
    coming["gram_line"] = lambda: wait_for(gram_line, line_recv.at[0])
    for s in SENDS["post"]:
        send_dosage(s)
    for g in ORDER:
        swap(g)
    for g in ORDER:
        turn(g)
    for g in range(4):
        multiply(g)

    for c in range(2):
        total = g_acc[c]
        g_half[c] = (total[:64, :128] + total[64:, 128:]) * scale
    g_copy = remote(g_half.at[other], g_own.at[core], g_send, g_recv, z, mate)
    g_copy.start()
    leaving.append(g_copy.wait_send)
    coming["g"] = g_copy.wait_recv
    g_own[core] = g_half[core]

    near, far = g_half[core], g_half[other]
    take("hist")
    sub = lax.broadcasted_iota(jnp.int32, (16, 128), 0)
    lane = lax.broadcasted_iota(jnp.int32, (16, 128), 1)
    folds = []
    for i in range(2 * PAIRS):
        both = hist[i, :, lanes].astype(jnp.float32) * near + hist_other[i].astype(jnp.float32) * far
        folds.append(jnp.sum(both, axis=0, keepdims=True))
    sums = jnp.sum(jnp.concatenate(folds, axis=0), axis=1, keepdims=True)
    dots_own[0] = jnp.sum(jnp.where(sub == lane, sums, 0.0), axis=0, keepdims=True)
    for s in range(1, ZN):
        remote(dots_own.at[0], dots_line.at[s - 1], line_send.at[1], line_recv.at[1], at_z(s), v).start()
    leaving.append(lambda: wait_for(dots_line, line_send.at[1]))
    coming["dots_line"] = lambda: wait_for(dots_line, line_recv.at[1])

    take("gram_line")
    scaling, rows = weight_rows(row_sum(gram_line[...]) + gram_own[1])
    gamma[...] = scaling
    for i in range(2 * PAIRS):
        weights[i : i + 1, :] = rows[i]
    take("g")

    take("dots_line")
    dots_mid[0] = row_sum(dots_line[...]) + dots_own[0]

    @pl.loop(1, VN)
    def _(r):
        remote(
            dots_mid.at[0], dots_plane.at[VN - 1 - r], dots_send, dots_recv, z, lax.rem(v + r, VN)
        ).start()

    leaving.append(lambda: wait_for(dots_plane, dots_send))
    coming["dots"] = lambda: wait_for(dots_plane, dots_recv)

    own_rows = pl.ds(pl.multiple_of(z * 64, 64), 64)
    start = coef[own_rows, :].astype(jnp.float32)
    gradient = jnp.concatenate([g_own[0], g_own[1]], axis=1)
    start = start - STEP * (gamma[0:1, 0:1] * gradient)
    limit = STEP * penalty_ref[...]

    take("dots")
    dots = row_sum(dots_plane[...]) + dots_mid[0]
    mix = jnp.sum(weights[...] * dots, axis=1, keepdims=True)
    along = mix[0:1] * hist[0].astype(jnp.float32)
    for i in range(1, 2 * PAIRS):
        along = along + mix[i : i + 1] * hist[i].astype(jnp.float32)
    moved = start - STEP * along
    out_ref[...] = moved - jnp.clip(moved, -limit, limit)
    finish()


def per_device(dosage, coefficients, targets, mask_words, penalty, past_steps, past_changes):
    samples, variants = dosage.shape
    traits = coefficients.shape[1]
    owned = variants // ZN
    f32, bf16 = jnp.float32, jnp.bfloat16
    vmem = pltpu.VMEM
    dma = pltpu.SemaphoreType.DMA
    anywhere = pl.BlockSpec(memory_space=pl.ANY)
    return pl.pallas_call(
        kernel,
        out_shape=jax.ShapeDtypeStruct((owned, traits), f32),
        in_specs=[anywhere] * 4 + [pl.BlockSpec(memory_space=vmem)] + [anywhere] * 2,
        out_specs=pl.BlockSpec(memory_space=vmem),
        scratch_shapes=[
            vmem((samples, variants), bf16),
            vmem((variants, traits), bf16),
            vmem((samples, traits), bf16),
            vmem(mask_words.shape[::-1], jnp.int32),
            vmem(mask_words.shape, f32),
            vmem((2 * PAIRS, owned, traits), bf16),
            vmem((UNITS, 2, 16, 128), f32),
            vmem((ZN, 96, 128), bf16),
            vmem((2, ZN, 96, 128), bf16),
            vmem((2, 4, 128, 384), bf16),
            vmem((ZN, UNITS, 16, 128), bf16),
            vmem((VN - 1, 16, 128), f32),
            vmem((2 * PAIRS, owned, 128), bf16),
            vmem((128, 8, 128), f32),
            vmem((2, 1, 128), f32),
            vmem((VN - 1, 1, 128), f32),
            vmem((ZN - 1, 1, 128), f32),
            vmem((2 * PAIRS, 128), f32),
            vmem((1, 128), f32),
            vmem((2, 128, 256), f32),
            vmem((2, owned, 128), f32),
            vmem((2, owned, 128), f32),
            vmem((1, 1, 128), f32),
            vmem((ZN - 1, 1, 128), f32),
            vmem((1, 1, 128), f32),
            vmem((VN - 1, 1, 128), f32),
            dma((6,)),
            dma,
            dma,
            dma,
            dma((4,)),
            dma,
            dma((4,)),
            dma,
            dma,
            dma,
            dma,
            dma((2,)),
            dma((2,)),
            dma((2,)),
            dma((9,)),
            dma,
            dma,
            dma,
            dma,
            pltpu.SemaphoreType.REGULAR,
        ],
        compiler_params=pltpu.CompilerParams(
            collective_id=0, has_side_effects=True, vmem_limit_bytes=55130 * 1024
        ),
    )(dosage, coefficients, targets, mask_words.T, penalty[None, :], past_steps, past_changes)


def solution(mesh):
    in_specs = (
        P("samp", "var"),
        P("var", None),
        P("samp", None),
        P("samp", None),
        P(),
        P(None, ("var", "samp"), None),
        P(None, ("var", "samp"), None),
    )
    out_specs = P(("var", "samp"), None)
    return jax.shard_map(
        per_device, mesh=mesh, in_specs=in_specs, out_specs=out_specs, check_vma=False
    )
```
